32 devices in a mesh: replica: 2 (over y), adapter: 4 (over z), tensor: 4 (over x, core).
Axes of the slice: x: 2, y: 2, z: 4, core: 2. Of those that a mesh axis runs over, the one named last changes fastest.
Arguments:
- tokens: bfloat16 [8192, 8192], P(('replica', 'adapter'), 'tensor'), parts along dimension 0, may hold values from -6 to 6
- value_base_matrix: bfloat16 [8192, 1024], P('tensor'), may hold values from -0.0625 to 0.0625
- adapter_down_table: bfloat16 [8, 8192, 64], P('adapter', 'tensor'), may hold values from -0.0625 to 0.0625
- adapter_up_table: bfloat16 [8, 64, 1024], P('adapter', None, 'tensor'), may hold values from -0.75 to 0.75
- adapter_per_block: int32 [128], P(('replica', 'adapter')), parts along dimension 0, may hold values from 0 to 7, as said below
- adapter_position: int32 [16], P('replica'), parts along dimension 0, may hold values from 0 to 7, as said below
Outputs:
- values_out: bfloat16 [8192, 1024], P(('replica', 'adapter'), 'tensor'), parts along dimension 0
The draws below stay inside these ranges and needn't reach their ends.
There are 2 independent parts, one for each index of `replica`. The reference program is written for one: setup_inputs(seed, part) draws one part's arguments, and reference() takes and returns one part's arrays. A program takes and returns all parts, laid end to end along the dimension named above; an argument that names none is the same for every part. Nothing has to cross between parts.
Inputs may be any that keep to these rules, and one draw needn't show every extreme that they name: A permutation: adapter a lives in slot adapter_position[a]. The owner of a slot s is s // 2. `adapter_per_block`: of the 16 blocks of one device, at most 4 belong to adapters of one owner; in every draw some owner gets exactly 4 blocks from every device.
All inputs are finite; a program needn't handle non-finite values.
Results may differ from the reference program's by a relative error of at most 0.014.
Values may be sent and summed in bfloat16 or wider, within the bound.
A program may use at most 64 MiB of HBM per device.

```python
import jax
import jax.numpy as jnp
from jax import lax

MODEL_WIDTH = 8192
VALUE_OUT_WIDTH = 1024
ADAPTER_RANK = 64
BLK = 64
ADP_DEV = 2
TOKEN_TOTAL = 4096
ADAPTER_TOTAL = 8
NBLK = 16
BLOCKS = 64
MOST = 4
N_ADAPTER = 4
N_TENSOR = 4


def slot_order(key):
    return jax.random.permutation(key, ADAPTER_TOTAL).astype(jnp.int32)


def draw_adapter_position(key, part):
    return slot_order(key)


def draw_adapter_per_block(key, part):
    slot_map = slot_order(key)
    key = jax.random.fold_in(key, 5)
    inverse = jnp.zeros((ADAPTER_TOTAL,), jnp.int32).at[slot_map].set(jnp.arange(ADAPTER_TOTAL, dtype=jnp.int32))
    hot_key, pool_key, local_key = jax.random.split(key, 3)
    hottest = jax.random.randint(hot_key, (), 0, N_ADAPTER).astype(jnp.int32)
    others = jnp.arange((N_ADAPTER - 1) * MOST, dtype=jnp.int32) // MOST
    others = others + (others >= hottest).astype(jnp.int32)

    def one_source(source_key):
        first_key, second_key = jax.random.split(source_key)
        picked = jax.random.permutation(first_key, others)[:NBLK - MOST]
        owners = jnp.concatenate([jnp.full((MOST,), hottest, jnp.int32), picked])
        return jax.random.permutation(second_key, owners)
    owner_rows = jax.vmap(one_source)(jax.random.split(pool_key, N_ADAPTER))
    local_rows = jax.random.randint(local_key, (N_ADAPTER, NBLK), 0, ADP_DEV).astype(jnp.int32)
    return inverse[owner_rows * ADP_DEV + local_rows].reshape(BLOCKS).astype(jnp.int32)


def steps_of(rng, shape, cuts, least, top_value):
    level, own = 1.0, jax.random.fold_in(rng, 6)
    for axis_at, parts in cuts:
        draws = jnp.exp(jax.random.uniform(jax.random.fold_in(own, axis_at), (parts,), jnp.float32, least / len(cuts), top_value / len(cuts)))
        level = level * jnp.repeat(draws, shape[axis_at] // parts).reshape([-1 if axis == axis_at else 1 for axis in range(len(shape))])
    return level


def gaussian(own_key, dims, deviation, reach, cuts=(), kind=jnp.bfloat16):
    loudness = steps_of(own_key, dims, cuts, -0.22, 0.18) if cuts else 1.0
    values = jax.random.normal(own_key, dims, jnp.float32) * deviation * loudness
    return jnp.minimum(jnp.maximum(values, -reach), reach).astype(kind)


def setup_inputs(seed: int = 0, part: int = 0) -> dict:
    keys = jax.random.split(jax.random.key(seed), 7)
    own_keys = jax.random.split(jax.random.fold_in(keys[6], part), 7)
    return {
        "tokens": gaussian(own_keys[0], (TOKEN_TOTAL, MODEL_WIDTH), 1.0, 6.0, ((0, 4), (1, 4))),
        "value_base_matrix": gaussian(keys[1], (MODEL_WIDTH, VALUE_OUT_WIDTH), MODEL_WIDTH ** -0.5, 0.0625, ((0, 4),)),
        "adapter_down_table": gaussian(keys[2], (ADAPTER_TOTAL, MODEL_WIDTH, ADAPTER_RANK), MODEL_WIDTH ** -0.5, 0.0625, ((0, 4), (1, 4))),
        "adapter_up_table": gaussian(keys[3], (ADAPTER_TOTAL, ADAPTER_RANK, VALUE_OUT_WIDTH), ADAPTER_RANK ** -0.5, 0.75, ((0, 4), (2, 4))),
        "adapter_per_block": draw_adapter_per_block(jax.random.fold_in(jax.random.fold_in(keys[6], part), 71), part),
        "adapter_position": draw_adapter_position(jax.random.fold_in(jax.random.fold_in(keys[6], part), 71), part),
    }


def reference(tokens, value_base_matrix, adapter_down_table, adapter_up_table, adapter_per_block, adapter_position):
    feat_width = MODEL_WIDTH // N_TENSOR
    base_projected = jnp.zeros((TOKEN_TOTAL, VALUE_OUT_WIDTH), jnp.float32)
    for index in range(N_TENSOR):
        partial_value = jnp.dot(tokens[:, index * feat_width:(index + 1) * feat_width], value_base_matrix[index * feat_width:(index + 1) * feat_width], preferred_element_type=jnp.float32)
        rounded = lax.optimization_barrier(partial_value.astype(jnp.bfloat16))
        base_projected = base_projected + rounded.astype(jnp.float32)
    slot_per_block = adapter_position[adapter_per_block].astype(jnp.int32)
    token_groups_list = tokens.reshape(BLOCKS, BLK, MODEL_WIDTH)

    def block_update(pair):
        block_rows, slot_position = pair
        down_matrix = lax.dynamic_index_in_dim(adapter_down_table, slot_position, 0, keepdims=False)
        up_matrix = lax.dynamic_index_in_dim(adapter_up_table, slot_position, 0, keepdims=False)
        shrunk = jnp.dot(block_rows, down_matrix, preferred_element_type=jnp.float32).astype(jnp.bfloat16)
        return jnp.dot(shrunk, up_matrix, preferred_element_type=jnp.float32).astype(jnp.bfloat16)

    adapter_update = lax.map(block_update, (token_groups_list, slot_per_block))
    adapter_update = lax.optimization_barrier(adapter_update.reshape(TOKEN_TOTAL, VALUE_OUT_WIDTH))
    return (base_projected + adapter_update.astype(jnp.float32)).astype(jnp.bfloat16)
```

```python
import functools

import jax
import jax.numpy as jnp
from jax import lax
from jax.experimental import pallas as pl
from jax.experimental.pallas import tpu as pltpu
from jax.sharding import PartitionSpec as P

BLK = 64
PIECES = 4
ROWS = 256
MESH = pl.DeviceIdType.MESH


def shards(
    tokens,
    value_base_matrix,
    adapter_down_table,
    adapter_up_table,
    adapter_per_block,
    adapter_position,
):
    partial_value = jnp.dot(tokens, value_base_matrix, preferred_element_type=jnp.float32)
    base_projected = lax.psum_scatter(
        partial_value.astype(jnp.bfloat16), "tensor", scatter_dimension=1, tiled=True
    ).astype(jnp.float32)
    feat_width = tokens.shape[1]
    block_count = tokens.shape[0] // BLK
    all_adapters = adapter_position.shape[0]
    output_width = adapter_up_table.shape[2]
    token_groups_list = tokens.reshape(block_count, BLK, feat_width)
    matches = adapter_per_block[:, None] == jnp.arange(all_adapters, dtype=jnp.int32)[None, :]
    slot_per_block = jnp.sum(jnp.where(matches, adapter_position[None, :], 0), axis=1)
    table_down, table_up = (
        lax.all_gather(adapter_down_table, "adapter", axis=0, tiled=True),
        lax.all_gather(adapter_up_table, "adapter", axis=0, tiled=True),
    )
    down_rows = table_down[slot_per_block]
    up_rows = table_up[slot_per_block]
    shrunk_part = jnp.einsum(
        "bnd,bdr->bnr", token_groups_list, down_rows, preferred_element_type=jnp.float32
    )
    shrunk = lax.psum(shrunk_part.astype(jnp.bfloat16), "tensor")
    adapter_update = jnp.einsum(
        "bnr,bro->bno", shrunk, up_rows, preferred_element_type=jnp.float32
    ).astype(jnp.bfloat16)
    adapter_update = lax.optimization_barrier(adapter_update.reshape(tokens.shape[0], output_width))
    return (base_projected + adapter_update.astype(jnp.float32)).astype(jnp.bfloat16)


def kernel(
    owners,
    apb,
    apos,
    tok_h,
    base_h,
    down_h,
    up_h,
    out,
    tok,
    base,
    table,
    toks,
    sib_send,
    sib_recv,
    x_send,
    x_recv,
    total,
    rank_f32,
    rank_send,
    rank_sib,
    rank_x_send,
    rank_x,
    delta,
    load_sem,
    z_recv,
    y_recv,
    right_sem,
    left_sem,
    y_send,
    base_sem,
    rank_sem,
):
    y = lax.axis_index("replica")
    z = lax.axis_index("adapter")
    t = lax.axis_index("tensor")
    core = lax.rem(t, 2)
    sibling = t + 1 - 2 * core
    far = lax.rem(t + 2, 4)
    other_y = 1 - y
    last = owners - 1

    blocks, _, feats = tok.shape
    quarter = out.shape[2]
    per_owner = blocks // owners
    owner_rows = per_owner * BLK
    half_feats = feats // 2
    width = 2 * BLK
    piece = width // PIECES

    loads = []
    for h in range(2):
        loads.append(pltpu.make_async_copy(
            up_h.at[:, h * width:(h + 1) * width], table.at[z, h, :, :width], load_sem.at[2 * h]))
        loads.append(pltpu.make_async_copy(
            down_h.at[:, h * half_feats:(h + 1) * half_feats], table.at[z, h, :, width:], load_sem.at[2 * h + 1]))
    loads.append(pltpu.make_async_copy(tok_h, tok, load_sem.at[4]))
    loads.append(pltpu.make_async_copy(base_h, base, load_sem.at[5]))
    for load in loads:
        load.start()

    barrier = pltpu.get_barrier_semaphore()

    def greet(where):
        pl.semaphore_signal(barrier, inc=1, device_id=where, device_id_type=MESH)

    greet({"tensor": sibling})
    greet({"tensor": far})
    greet({"replica": other_y})

    @pl.when(z > 0)
    def _():
        greet({"adapter": z - 1})

    @pl.when(z < last)
    def _():
        greet({"adapter": z + 1})

    for load in loads[:4]:
        load.wait()
    neighbours = jnp.minimum(z, 1) + jnp.minimum(last - z, 1)
    pl.semaphore_wait(barrier, 3 + neighbours)

    def part(owner, half, p):
        return table.at[owner, half, p * piece:(p + 1) * piece, :]

    def z_copy(owner, p, to, send):
        ref = part(owner, y, p)
        return pltpu.make_async_remote_copy(
            src_ref=ref, dst_ref=ref, send_sem=send.at[owner, p], recv_sem=z_recv.at[owner, p],
            device_id={"adapter": to}, device_id_type=MESH,
        )

    def y_copy(owner, p, half):
        ref = part(owner, half, p)
        return pltpu.make_async_remote_copy(
            src_ref=ref, dst_ref=ref, send_sem=y_send.at[owner, p], recv_sem=y_recv.at[owner, p],
            device_id={"replica": other_y}, device_id_type=MESH,
        )

    for p in range(PIECES):
        @pl.when(z < last)
        def _():
            z_copy(z, p, z + 1, right_sem).start()

        @pl.when(z > 0)
        def _():
            z_copy(z, p, z - 1, left_sem).start()

    def forward(distance, p):
        @pl.when(z >= distance)
        def _():
            owner = z - distance
            z_copy(owner, p, z - 1, right_sem).wait_recv()

            @pl.when(z < last)
            def _():
                z_copy(owner, p, z + 1, right_sem).start()
            y_copy(owner, p, y).start()

        @pl.when(z + distance <= last)
        def _():
            owner = z + distance
            z_copy(owner, p, z + 1, left_sem).wait_recv()

            @pl.when(z > 0)
            def _():
                z_copy(owner, p, z - 1, left_sem).start()
            y_copy(owner, p, y).start()

    def same(a, b):
        return 1 - jnp.minimum((a - b) * (a - b), 1)

    slot = [apos[apb[b]] for b in range(blocks)]
    owner_of = [lax.div(s, 2) for s in slot]
    place = []
    for b in range(blocks):
        before = jnp.int32(0)
        for c in range(b):
            before = before + same(owner_of[c], owner_of[b])
        place.append(owner_of[b] * per_owner + before)

    row_blocks = ROWS // BLK
    row_steps = blocks // row_blocks

    def base_piece(column, r):
        at = pl.ds(r * row_blocks, row_blocks)
        columns = pl.ds(pl.multiple_of(column * quarter, quarter), quarter)
        rows = tok[at].reshape(ROWS, feats)
        value = jnp.dot(rows, base[:, columns], preferred_element_type=jnp.float32)
        return at, value.reshape(row_blocks, BLK, quarter)

    def base_copy(src, dst, sem, to):
        return pltpu.make_async_remote_copy(
            src_ref=src, dst_ref=dst, send_sem=base_sem.at[2 * sem], recv_sem=base_sem.at[2 * sem + 1],
            device_id={"tensor": to}, device_id_type=MESH,
        )

    sib_copy = [base_copy(sib_send.at[i], sib_recv.at[i], i, sibling) for i in range(2)]
    x_copy = base_copy(x_send, x_recv, 2, far)

    loads[4].wait()
    loads[5].wait()

    far_sibling = far + 1 - 2 * core

    @pl.loop(0, row_steps)
    def _(r):
        at, value = base_piece(far_sibling, r)
        sib_send[0, at] = value.astype(jnp.bfloat16)
    sib_copy[0].start()
    forward(1, 0)

    @pl.loop(0, row_steps)
    def _(r):
        at, value = base_piece(far, r)
        total[at] = value
    sib_copy[0].wait_recv()
    x_send[...] = (total[...] + sib_recv[0].astype(jnp.float32)).astype(jnp.bfloat16)
    x_copy.start()
    forward(1, 1)

    @pl.loop(0, row_steps)
    def _(r):
        at, value = base_piece(sibling, r)
        sib_send[1, at] = value.astype(jnp.bfloat16)
    sib_copy[1].start()
    forward(1, 2)

    @pl.loop(0, row_steps)
    def _(r):
        at, value = base_piece(t, r)
        total[at] = value
    for p in range(3, PIECES):
        forward(1, p)

    parity = []
    for s in range(blocks):
        index, odd = jnp.int32(0), jnp.int32(0)
        for b in range(blocks):
            here = same(place[b], s)
            index = index + here * b
            odd = odd + here * lax.rem(slot[b], 2)
        parity.append(odd)
        toks[s] = tok[index]

    lane_half = lax.div(lax.broadcasted_iota(jnp.int32, (BLK, width), 1), BLK)

    def own_lanes(owner, k):
        odd = jnp.int32(0)
        for o in range(owners):
            odd = odd + same(owner, o) * parity[o * per_owner + k]
        return same(lane_half, odd).astype(jnp.float32)

    def rank_copy(src, dst, owner, kind, to):
        return pltpu.make_async_remote_copy(
            src_ref=src.at[owner], dst_ref=dst.at[owner],
            send_sem=rank_sem.at[2 * kind, owner], recv_sem=rank_sem.at[2 * kind + 1, owner],
            device_id={"tensor": to}, device_id_type=MESH,
        )

    pairs = per_owner // 2

    def shrink(owner):
        rows = toks[pl.ds(owner * per_owner, per_owner)].reshape(owner_rows, feats)
        value = jnp.zeros((owner_rows, width), jnp.float32)
        for h in range(2):
            value = value + lax.dot_general(
                rows[:, h * half_feats:(h + 1) * half_feats], table[owner, h, :, width:],
                (((1,), (1,)), ((), ())), preferred_element_type=jnp.float32,
            )
        picked = []
        for k in range(per_owner):
            rank = value[k * BLK:(k + 1) * BLK, :] * own_lanes(owner, k)
            picked.append(rank[:, :BLK] + rank[:, BLK:])
        packed = jnp.concatenate(
            [jnp.concatenate(picked[:pairs], axis=0), jnp.concatenate(picked[pairs:], axis=0)], axis=1
        )
        rank_f32[owner] = packed
        rank_send[owner] = packed.astype(jnp.bfloat16)
        rank_copy(rank_send, rank_sib, owner, 0, sibling).start()

    def chip_sum(owner):
        rank_copy(rank_send, rank_sib, owner, 0, sibling).wait_recv()
        value = rank_f32[owner] + rank_sib[owner].astype(jnp.float32)
        rank_f32[owner] = value
        rank_x_send[owner] = value.astype(jnp.bfloat16)
        rank_copy(rank_x_send, rank_x, owner, 1, far).start()

    def expand(owner):
        rank_copy(rank_x_send, rank_x, owner, 1, far).wait_recv()
        value = rank_f32[owner] + rank_x[owner].astype(jnp.float32)
        spread = []
        for k in range(per_owner):
            column = (k // pairs) * BLK
            rank = value[(k % pairs) * BLK:(k % pairs + 1) * BLK, column:column + BLK]
            spread.append(jnp.concatenate([rank, rank], axis=1) * own_lanes(owner, k))
        shrunk = jnp.concatenate(spread, axis=0).astype(jnp.bfloat16)
        for h in range(2):
            value = jnp.dot(shrunk, table[owner, h, :, :width], preferred_element_type=jnp.float32)
            delta[pl.ds(owner * per_owner, per_owner), :, h * width:(h + 1) * width] = value.reshape(
                per_owner, BLK, width
            )

    order = [z]
    for j in range(1, owners):
        pick = jnp.int32(0)
        for me in range(owners):
            by_distance = sorted((o for o in range(owners) if o != me), key=lambda o: abs(o - me))
            pick = jnp.where(z == me, by_distance[j - 1], pick)
        order.append(pick)

    def y_wait(owner):
        for p in range(PIECES):
            y_copy(owner, p, other_y).wait_recv()

    shrink(order[0])
    for p in range(PIECES):
        forward(2, p)
        if p == 0:
            chip_sum(order[0])
        if p == 1:
            expand(order[0])
    y_wait(order[1])
    shrink(order[1])
    forward(3, 0)
    chip_sum(order[1])
    y_wait(order[2])
    shrink(order[2])
    forward(3, 1)
    expand(order[1])
    chip_sum(order[2])
    forward(3, 2)
    sib_copy[1].wait_recv()
    x_copy.wait_recv()
    total[...] = total[...] + sib_recv[1].astype(jnp.float32) + x_recv[...].astype(jnp.float32)
    for p in range(3, PIECES):
        forward(3, p)
    expand(order[2])
    y_wait(order[3])
    shrink(order[3])
    chip_sum(order[3])
    expand(order[3])
    for b in range(blocks):
        out[b] = (total[b] + delta[place[b]]).astype(jnp.bfloat16)

    for copy in (*sib_copy, x_copy):
        copy.wait_send()
    for owner in range(owners):
        rank_copy(rank_send, rank_sib, owner, 0, sibling).wait_send()
        rank_copy(rank_x_send, rank_x, owner, 1, far).wait_send()
        for p in range(PIECES):
            @pl.when(owner != z)
            def _():
                y_copy(owner, p, y).wait_send()

            @pl.when(jnp.logical_and(owner <= z, z < last))
            def _():
                z_copy(owner, p, z + 1, right_sem).wait_send()

            @pl.when(jnp.logical_and(owner >= z, z > 0))
            def _():
                z_copy(owner, p, z - 1, left_sem).wait_send()


def fused(owners, tokens, value_base_matrix, down_table, up_table, adapter_per_block, adapter_position):
    rows, feats = tokens.shape
    quarter = up_table.shape[2]
    out_columns = value_base_matrix.shape[1]
    width = 2 * BLK
    blocks = rows // BLK
    owner_rows = rows // owners
    tokens = tokens.reshape(blocks, BLK, feats)
    down_rows = down_table.transpose(0, 2, 1).reshape(width, feats)
    up_rows = up_table.reshape(width, quarter)
    by_block = (blocks, BLK, quarter)
    any_spec = pl.BlockSpec(memory_space=pl.ANY)
    smem = pl.BlockSpec(memory_space=pltpu.SMEM)
    rank_shape = (owners, owner_rows // 2, width)
    dma = pltpu.SemaphoreType.DMA
    out = pl.pallas_call(
        functools.partial(kernel, owners),
        out_shape=jax.ShapeDtypeStruct(by_block, jnp.bfloat16),
        in_specs=[smem, smem, any_spec, any_spec, any_spec, any_spec],
        out_specs=pl.BlockSpec(memory_space=pltpu.VMEM),
        scratch_shapes=[
            pltpu.VMEM((blocks, BLK, feats), jnp.bfloat16),
            pltpu.VMEM((feats, out_columns), jnp.bfloat16),
            pltpu.VMEM((owners, 2, width, width + feats // 2), jnp.bfloat16),
            pltpu.VMEM((blocks, BLK, feats), jnp.bfloat16),
            pltpu.VMEM((2, *by_block), jnp.bfloat16),
            pltpu.VMEM((2, *by_block), jnp.bfloat16),
            pltpu.VMEM(by_block, jnp.bfloat16),
            pltpu.VMEM(by_block, jnp.bfloat16),
            pltpu.VMEM(by_block, jnp.float32),
            pltpu.VMEM(rank_shape, jnp.float32),
            pltpu.VMEM(rank_shape, jnp.bfloat16),
            pltpu.VMEM(rank_shape, jnp.bfloat16),
            pltpu.VMEM(rank_shape, jnp.bfloat16),
            pltpu.VMEM(rank_shape, jnp.bfloat16),
            pltpu.VMEM(by_block, jnp.float32),
            dma((6,)),
            dma((owners, PIECES)),
            dma((owners, PIECES)),
            dma((owners, PIECES)),
            dma((owners, PIECES)),
            dma((owners, PIECES)),
            dma((6,)),
            dma((4, owners)),
        ],
        compiler_params=pltpu.CompilerParams(
            collective_id=0, has_side_effects=True, vmem_limit_bytes=48 * 1024 * 1024
        ),
        cost_estimate=pl.CostEstimate(
            flops=2 * rows * feats * (out_columns + width),
            bytes_accessed=2 * (rows * feats + feats * out_columns + rows * quarter),
            transcendentals=0,
        ),
    )(adapter_per_block, adapter_position, tokens, value_base_matrix, down_rows, up_rows)
    return out.reshape(rows, quarter)


def solution(mesh):
    axes = mesh.shape

    def run(tokens, value_base_matrix, down_table, up_table, adapter_per_block, adapter_position):
        fits = (
            axes["tensor"] == 4
            and axes["replica"] == 2
            and axes["adapter"] == 4
            and down_table.shape[0] == 2
            and tokens.shape[0] == 16 * BLK
            and up_table.shape[1:] == (BLK, 4 * BLK)
            and tokens.shape[1] % 512 == 0
        )
        if fits:
            return fused(
                axes["adapter"], tokens, value_base_matrix, down_table, up_table, adapter_per_block, adapter_position
            )
        return shards(tokens, value_base_matrix, down_table, up_table, adapter_per_block, adapter_position)

    return jax.shard_map(
        run,
        mesh=mesh,
        in_specs=(
            P(("replica", "adapter"), "tensor"),
            P("tensor", None),
            P("adapter", "tensor", None),
            P("adapter", None, "tensor"),
            P(("replica", "adapter")),
            P("replica"),
        ),
        out_specs=P(("replica", "adapter"), "tensor"),
        check_vma=False,
    )
```

```python
import functools

import jax
import jax.numpy as jnp
from jax import lax
from jax.experimental import pallas as pl
from jax.experimental.pallas import tpu as pltpu
from jax.sharding import PartitionSpec as P

BLK = 64
PIECES = 4
ROWS = 512
MESH = pl.DeviceIdType.MESH


def shards(
    tokens,
    value_base_matrix,
    adapter_down_table,
    adapter_up_table,
    adapter_per_block,
    adapter_position,
):
    partial_value = jnp.dot(tokens, value_base_matrix, preferred_element_type=jnp.float32)
    base_projected = lax.psum_scatter(
        partial_value.astype(jnp.bfloat16), "tensor", scatter_dimension=1, tiled=True
    ).astype(jnp.float32)
    feat_width = tokens.shape[1]
    block_count = tokens.shape[0] // BLK
    all_adapters = adapter_position.shape[0]
    output_width = adapter_up_table.shape[2]
    token_groups_list = tokens.reshape(block_count, BLK, feat_width)
    matches = adapter_per_block[:, None] == jnp.arange(all_adapters, dtype=jnp.int32)[None, :]
    slot_per_block = jnp.sum(jnp.where(matches, adapter_position[None, :], 0), axis=1)
    table_down, table_up = (
        lax.all_gather(adapter_down_table, "adapter", axis=0, tiled=True),
        lax.all_gather(adapter_up_table, "adapter", axis=0, tiled=True),
    )
    down_rows = table_down[slot_per_block]
    up_rows = table_up[slot_per_block]
    shrunk_part = jnp.einsum(
        "bnd,bdr->bnr", token_groups_list, down_rows, preferred_element_type=jnp.float32
    )
    shrunk = lax.psum(shrunk_part.astype(jnp.bfloat16), "tensor")
    adapter_update = jnp.einsum(
        "bnr,bro->bno", shrunk, up_rows, preferred_element_type=jnp.float32
    ).astype(jnp.bfloat16)
    adapter_update = lax.optimization_barrier(adapter_update.reshape(tokens.shape[0], output_width))
    return (base_projected + adapter_update.astype(jnp.float32)).astype(jnp.bfloat16)


def kernel(
    owners,
    apb_h,
    apos_h,
    tok_h,
    base_h,
    down_h,
    up_h,
    out,
    tok,
    base,
    table,
    toks,
    sib_send,
    sib_recv,
    x_send,
    x_recv,
    total,
    rank_f32,
    rank_send,
    rank_sib,
    rank_x_send,
    rank_x,
    last_recv,
    delta,
    apb,
    apos,
    load_sem,
    z_recv,
    y_recv,
    right_sem,
    left_sem,
    y_send,
    base_sem,
    rank_sem,
    last_sem,
):
    y = lax.axis_index("replica")
    z = lax.axis_index("adapter")
    t = lax.axis_index("tensor")
    core = lax.rem(t, 2)
    sibling = t + 1 - 2 * core
    far = lax.rem(t + 2, 4)
    far_sibling = far + 1 - 2 * core
    other_y = 1 - y
    last = owners - 1

    blocks, _, feats = tok.shape
    quarter = out.shape[2]
    per_owner = blocks // owners
    owner_rows = per_owner * BLK
    half_feats = feats // 2
    width = 2 * BLK
    piece = width // PIECES

    loads = []
    for h in range(2):
        loads.append(pltpu.make_async_copy(
            up_h.at[:, h * width:(h + 1) * width], table.at[z, h, :, :width], load_sem.at[2 * h]))
        loads.append(pltpu.make_async_copy(
            down_h.at[:, h * half_feats:(h + 1) * half_feats], table.at[z, h, :, width:], load_sem.at[2 * h + 1]))
    loads.append(pltpu.make_async_copy(tok_h, tok, load_sem.at[4]))
    loads.append(pltpu.make_async_copy(base_h, base, load_sem.at[5]))
    loads.append(pltpu.make_async_copy(apb_h, apb, load_sem.at[6]))
    loads.append(pltpu.make_async_copy(apos_h, apos, load_sem.at[7]))
    for load in loads:
        load.start()

    barrier = pltpu.get_barrier_semaphore()

    def greet(where):
        pl.semaphore_signal(barrier, inc=1, device_id=where, device_id_type=MESH)

    greet({"tensor": sibling})
    greet({"tensor": far})
    greet({"tensor": far_sibling})
    greet({"replica": other_y})

    @pl.when(z > 0)
    def _():
        greet({"adapter": z - 1})

    @pl.when(z < last)
    def _():
        greet({"adapter": z + 1})

    for load in loads[:4]:
        load.wait()
    neighbours = jnp.minimum(z, 1) + jnp.minimum(last - z, 1)
    pl.semaphore_wait(barrier, 4 + neighbours)

    def part(owner, half, p):
        return table.at[owner, half, p * piece:(p + 1) * piece, :]

    def z_copy(owner, p, to, send):
        ref = part(owner, y, p)
        return pltpu.make_async_remote_copy(
            src_ref=ref, dst_ref=ref, send_sem=send.at[owner, p], recv_sem=z_recv.at[owner, p],
            device_id={"adapter": to}, device_id_type=MESH,
        )

    def y_copy(owner, p, half):
        ref = part(owner, half, p)
        return pltpu.make_async_remote_copy(
            src_ref=ref, dst_ref=ref, send_sem=y_send.at[owner, p], recv_sem=y_recv.at[owner, p],
            device_id={"replica": other_y}, device_id_type=MESH,
        )

    for p in range(PIECES):
        @pl.when(z < last)
        def _():
            z_copy(z, p, z + 1, right_sem).start()

        @pl.when(z > 0)
        def _():
            z_copy(z, p, z - 1, left_sem).start()

    def forward(distance, p):
        @pl.when(z >= distance)
        def _():
            owner = z - distance
            z_copy(owner, p, z - 1, right_sem).wait_recv()

            @pl.when(z < last)
            def _():
                z_copy(owner, p, z + 1, right_sem).start()
            y_copy(owner, p, y).start()

        @pl.when(z + distance <= last)
        def _():
            owner = z + distance
            z_copy(owner, p, z + 1, left_sem).wait_recv()

            @pl.when(z > 0)
            def _():
                z_copy(owner, p, z - 1, left_sem).start()
            y_copy(owner, p, y).start()

    def same(a, b):
        return 1 - jnp.minimum((a - b) * (a - b), 1)

    loads[6].wait()
    loads[7].wait()
    slot = [apos[apb[b]] for b in range(blocks)]
    owner_of = [lax.div(s, 2) for s in slot]
    place = []
    for b in range(blocks):
        before = jnp.int32(0)
        for c in range(b):
            before = before + same(owner_of[c], owner_of[b])
        place.append(owner_of[b] * per_owner + before)

    row_blocks = ROWS // BLK
    row_steps = blocks // row_blocks

    def base_piece(column, r):
        at = pl.ds(r * row_blocks, row_blocks)
        columns = pl.ds(pl.multiple_of(column * quarter, quarter), quarter)
        rows = tok[at].reshape(ROWS, feats)
        value = jnp.dot(rows, base[:, columns], preferred_element_type=jnp.float32)
        return at, value.reshape(row_blocks, BLK, quarter)

    def base_copy(src, dst, sem, to):
        return pltpu.make_async_remote_copy(
            src_ref=src, dst_ref=dst, send_sem=base_sem.at[2 * sem], recv_sem=base_sem.at[2 * sem + 1],
            device_id={"tensor": to}, device_id_type=MESH,
        )

    halves = [pl.ds(i * row_blocks, row_blocks) for i in range(row_steps)]
    far_sib_copy = [
        base_copy(sib_send.at[0, half], sib_recv.at[0, half], i, sibling) for i, half in enumerate(halves)
    ]
    x_copy = [base_copy(x_send.at[half], x_recv.at[half], row_steps + i, far) for i, half in enumerate(halves)]
    sib_copy = base_copy(sib_send.at[1], sib_recv.at[1], 2 * row_steps, sibling)

    loads[4].wait()
    loads[5].wait()

    for i in range(row_steps):
        at, value = base_piece(far_sibling, i)
        sib_send[0, at] = value.astype(jnp.bfloat16)
        far_sib_copy[i].start()
    forward(1, 0)
    for i in range(row_steps):
        at, value = base_piece(far, i)
        far_sib_copy[i].wait_recv()
        x_send[at] = (value + sib_recv[0, at].astype(jnp.float32)).astype(jnp.bfloat16)
        x_copy[i].start()
        forward(1, 1 + i)

    at, value = base_piece(sibling, 0)
    sib_send[1, at] = value.astype(jnp.bfloat16)
    for p in range(1 + row_steps, PIECES):
        forward(1, p)
    for i in range(1, row_steps):
        at, value = base_piece(sibling, i)
        sib_send[1, at] = value.astype(jnp.bfloat16)
    sib_copy.start()

    parity = []
    for s in range(blocks):
        index, odd = jnp.int32(0), jnp.int32(0)
        for b in range(blocks):
            here = same(place[b], s)
            index = index + here * b
            odd = odd + here * lax.rem(slot[b], 2)
        parity.append(odd)
        toks[s] = tok[index]

    lane_half = lax.div(lax.broadcasted_iota(jnp.int32, (BLK, width), 1), BLK)

    def own_lanes(owner, k):
        odd = jnp.int32(0)
        for o in range(owners):
            odd = odd + same(owner, o) * parity[o * per_owner + k]
        return same(lane_half, odd).astype(jnp.float32)

    def rank_copy(src, dst, owner, kind, to):
        return pltpu.make_async_remote_copy(
            src_ref=src.at[owner], dst_ref=dst.at[owner],
            send_sem=rank_sem.at[2 * kind, owner], recv_sem=rank_sem.at[2 * kind + 1, owner],
            device_id={"tensor": to}, device_id_type=MESH,
        )

    pairs = per_owner // 2

    def last_copies(owner):
        return [
            pltpu.make_async_remote_copy(
                src_ref=rank_send.at[owner], dst_ref=last_recv.at[i],
                send_sem=last_sem.at[2 * i], recv_sem=last_sem.at[2 * i + 1],
                device_id={"tensor": to}, device_id_type=MESH,
            )
            for i, to in enumerate((far_sibling, far, sibling))
        ]

    def shrink(owner, in_one_step=False):
        rows = toks[pl.ds(owner * per_owner, per_owner)].reshape(owner_rows, feats)
        value = jnp.zeros((owner_rows, width), jnp.float32)
        for h in range(2):
            value = value + lax.dot_general(
                rows[:, h * half_feats:(h + 1) * half_feats], table[owner, h, :, width:],
                (((1,), (1,)), ((), ())), preferred_element_type=jnp.float32,
            )
        picked = []
        for k in range(per_owner):
            rank = value[k * BLK:(k + 1) * BLK, :] * own_lanes(owner, k)
            picked.append(rank[:, :BLK] + rank[:, BLK:])
        packed = jnp.concatenate(
            [jnp.concatenate(picked[:pairs], axis=0), jnp.concatenate(picked[pairs:], axis=0)], axis=1
        )
        rank_f32[owner] = packed
        rank_send[owner] = packed.astype(jnp.bfloat16)
        if in_one_step:
            for copy in last_copies(owner):
                copy.start()
        else:
            rank_copy(rank_send, rank_sib, owner, 0, sibling).start()

    def chip_sum(owner):
        rank_copy(rank_send, rank_sib, owner, 0, sibling).wait_recv()
        value = rank_f32[owner] + rank_sib[owner].astype(jnp.float32)
        rank_f32[owner] = value
        rank_x_send[owner] = value.astype(jnp.bfloat16)
        rank_copy(rank_x_send, rank_x, owner, 1, far).start()

    def expand(owner, in_one_step=False):
        if in_one_step:
            for copy in last_copies(owner):
                copy.wait_recv()
            value = rank_f32[owner]
            for i in range(3):
                value = value + last_recv[i].astype(jnp.float32)
        else:
            rank_copy(rank_x_send, rank_x, owner, 1, far).wait_recv()
            value = rank_f32[owner] + rank_x[owner].astype(jnp.float32)
        spread = []
        for k in range(per_owner):
            column = (k // pairs) * BLK
            rank = value[(k % pairs) * BLK:(k % pairs + 1) * BLK, column:column + BLK]
            spread.append(jnp.concatenate([rank, rank], axis=1) * own_lanes(owner, k))
        shrunk = jnp.concatenate(spread, axis=0).astype(jnp.bfloat16)
        for h in range(2):
            value = jnp.dot(shrunk, table[owner, h, :, :width], preferred_element_type=jnp.float32)
            delta[pl.ds(owner * per_owner, per_owner), :, h * width:(h + 1) * width] = value.reshape(
                per_owner, BLK, width
            )

    order = [z]
    for j in range(1, owners):
        pick = jnp.int32(0)
        for me in range(owners):
            by_distance = sorted((o for o in range(owners) if o != me), key=lambda o: abs(o - me))
            pick = jnp.where(z == me, by_distance[j - 1], pick)
        order.append(pick)

    def y_wait(owner):
        for p in range(PIECES):
            y_copy(owner, p, other_y).wait_recv()

    forward(2, 0)
    shrink(order[0])
    forward(2, 1)
    for i in range(row_steps):
        at, value = base_piece(t, i)
        total[at] = value
        forward(2, 2 + i)
    for p in range(2 + row_steps, PIECES):
        forward(2, p)
    chip_sum(order[0])
    y_wait(order[1])
    shrink(order[1])
    sib_copy.wait_recv()
    total[...] = total[...] + sib_recv[1].astype(jnp.float32)
    forward(3, 0)
    expand(order[0])
    chip_sum(order[1])
    forward(3, 1)
    y_wait(order[2])
    shrink(order[2])
    forward(3, 2)
    expand(order[1])
    for p in range(3, PIECES):
        forward(3, p)
    chip_sum(order[2])
    for i, half in enumerate(halves):
        x_copy[i].wait_recv()
        total[half] = total[half] + x_recv[half].astype(jnp.float32)
    y_wait(order[3])
    shrink(order[3], in_one_step=True)
    expand(order[2])
    expand(order[3], in_one_step=True)
    for b in range(blocks):
        out[b] = (total[b] + delta[place[b]]).astype(jnp.bfloat16)

    for copy in (*far_sib_copy, *x_copy, sib_copy, *last_copies(order[3])):
        copy.wait_send()
    for owner in order[:3]:
        rank_copy(rank_send, rank_sib, owner, 0, sibling).wait_send()
        rank_copy(rank_x_send, rank_x, owner, 1, far).wait_send()
    for owner in range(owners):
        for p in range(PIECES):
            @pl.when(owner != z)
            def _():
                y_copy(owner, p, y).wait_send()

            @pl.when(jnp.logical_and(owner <= z, z < last))
            def _():
                z_copy(owner, p, z + 1, right_sem).wait_send()

            @pl.when(jnp.logical_and(owner >= z, z > 0))
            def _():
                z_copy(owner, p, z - 1, left_sem).wait_send()


def fused(owners, tokens, value_base_matrix, down_table, up_table, adapter_per_block, adapter_position):
    rows, feats = tokens.shape
    quarter = up_table.shape[2]
    out_columns = value_base_matrix.shape[1]
    width = 2 * BLK
    blocks = rows // BLK
    owner_rows = rows // owners
    tokens = tokens.reshape(blocks, BLK, feats)
    down_rows = down_table.transpose(0, 2, 1).reshape(width, feats)
    up_rows = up_table.reshape(width, quarter)
    by_block = (blocks, BLK, quarter)
    hbm = pl.BlockSpec(memory_space=pltpu.HBM)
    rank_shape = (owners, owner_rows // 2, width)
    dma = pltpu.SemaphoreType.DMA
    out = pl.pallas_call(
        functools.partial(kernel, owners),
        out_shape=jax.ShapeDtypeStruct(by_block, jnp.bfloat16),
        in_specs=[hbm] * 6,
        out_specs=pl.BlockSpec(memory_space=pltpu.VMEM),
        scratch_shapes=[
            pltpu.VMEM((blocks, BLK, feats), jnp.bfloat16),
            pltpu.VMEM((feats, out_columns), jnp.bfloat16),
            pltpu.VMEM((owners, 2, width, width + feats // 2), jnp.bfloat16),
            pltpu.VMEM((blocks, BLK, feats), jnp.bfloat16),
            pltpu.VMEM((2, *by_block), jnp.bfloat16),
            pltpu.VMEM((2, *by_block), jnp.bfloat16),
            pltpu.VMEM(by_block, jnp.bfloat16),
            pltpu.VMEM(by_block, jnp.bfloat16),
            pltpu.VMEM(by_block, jnp.float32),
            pltpu.VMEM(rank_shape, jnp.float32),
            pltpu.VMEM(rank_shape, jnp.bfloat16),
            pltpu.VMEM(rank_shape, jnp.bfloat16),
            pltpu.VMEM(rank_shape, jnp.bfloat16),
            pltpu.VMEM(rank_shape, jnp.bfloat16),
            pltpu.VMEM((3, *rank_shape[1:]), jnp.bfloat16),
            pltpu.VMEM(by_block, jnp.float32),
            pltpu.SMEM(adapter_per_block.shape, jnp.int32),
            pltpu.SMEM(adapter_position.shape, jnp.int32),
            dma((8,)),
            dma((owners, PIECES)),
            dma((owners, PIECES)),
            dma((owners, PIECES)),
            dma((owners, PIECES)),
            dma((owners, PIECES)),
            dma((2 * (2 * rows // ROWS + 1),)),
            dma((4, owners)),
            dma((6,)),
        ],
        compiler_params=pltpu.CompilerParams(
            collective_id=0, has_side_effects=True, vmem_limit_bytes=64 * 1024 * 1024
        ),
        cost_estimate=pl.CostEstimate(
            flops=2 * rows * feats * (out_columns + width),
            bytes_accessed=2 * (rows * feats + feats * out_columns + rows * quarter),
            transcendentals=0,
        ),
    )(adapter_per_block, adapter_position, tokens, value_base_matrix, down_rows, up_rows)
    return out.reshape(rows, quarter)


def solution(mesh):
    axes = mesh.shape

    def run(tokens, value_base_matrix, down_table, up_table, adapter_per_block, adapter_position):
        fits = (
            axes["tensor"] == 4
            and axes["replica"] == 2
            and axes["adapter"] == 4
            and down_table.shape[0] == 2
            and tokens.shape[0] == 16 * BLK
            and up_table.shape[1:] == (BLK, 4 * BLK)
            and tokens.shape[1] % 512 == 0
        )
        if fits:
            return fused(
                axes["adapter"], tokens, value_base_matrix, down_table, up_table, adapter_per_block, adapter_position
            )
        return shards(tokens, value_base_matrix, down_table, up_table, adapter_per_block, adapter_position)

    return jax.shard_map(
        run,
        mesh=mesh,
        in_specs=(
            P(("replica", "adapter"), "tensor"),
            P("tensor", None),
            P("adapter", "tensor", None),
            P("adapter", None, "tensor"),
            P(("replica", "adapter")),
            P("replica"),
        ),
        out_specs=P(("replica", "adapter"), "tensor"),
        check_vma=False,
    )
```

```python
import functools

import jax
import jax.numpy as jnp
from jax import lax
from jax.experimental import pallas as pl
from jax.experimental.pallas import tpu as pltpu
from jax.sharding import PartitionSpec as P

BLK = 64
PIECES = 4
ROWS = 512
MESH = pl.DeviceIdType.MESH


def shards(
    tokens,
    value_base_matrix,
    adapter_down_table,
    adapter_up_table,
    adapter_per_block,
    adapter_position,
):
    partial_value = jnp.dot(tokens, value_base_matrix, preferred_element_type=jnp.float32)
    base_projected = lax.psum_scatter(
        partial_value.astype(jnp.bfloat16), "tensor", scatter_dimension=1, tiled=True
    ).astype(jnp.float32)
    feat_width = tokens.shape[1]
    block_count = tokens.shape[0] // BLK
    all_adapters = adapter_position.shape[0]
    output_width = adapter_up_table.shape[2]
    token_groups_list = tokens.reshape(block_count, BLK, feat_width)
    matches = adapter_per_block[:, None] == jnp.arange(all_adapters, dtype=jnp.int32)[None, :]
    slot_per_block = jnp.sum(jnp.where(matches, adapter_position[None, :], 0), axis=1)
    table_down, table_up = (
        lax.all_gather(adapter_down_table, "adapter", axis=0, tiled=True),
        lax.all_gather(adapter_up_table, "adapter", axis=0, tiled=True),
    )
    down_rows = table_down[slot_per_block]
    up_rows = table_up[slot_per_block]
    shrunk_part = jnp.einsum(
        "bnd,bdr->bnr", token_groups_list, down_rows, preferred_element_type=jnp.float32
    )
    shrunk = lax.psum(shrunk_part.astype(jnp.bfloat16), "tensor")
    adapter_update = jnp.einsum(
        "bnr,bro->bno", shrunk, up_rows, preferred_element_type=jnp.float32
    ).astype(jnp.bfloat16)
    adapter_update = lax.optimization_barrier(adapter_update.reshape(tokens.shape[0], output_width))
    return (base_projected + adapter_update.astype(jnp.float32)).astype(jnp.bfloat16)


def kernel(
    owners,
    apb_h,
    apos_h,
    tok_h,
    base_h,
    down_h,
    up_h,
    out,
    tok,
    base,
    table,
    toks,
    sib_send,
    sib_recv,
    x_send,
    x_recv,
    total,
    rank_f32,
    rank_send,
    rank_sib,
    rank_x_send,
    rank_x,
    last_recv,
    delta,
    apb,
    apos,
    load_sem,
    z_recv,
    y_recv,
    right_sem,
    left_sem,
    y_send,
    base_sem,
    rank_sem,
    last_sem,
):
    y = lax.axis_index("replica")
    z = lax.axis_index("adapter")
    t = lax.axis_index("tensor")
    core = lax.rem(t, 2)
    sibling = t + 1 - 2 * core
    far = lax.rem(t + 2, 4)
    far_sibling = far + 1 - 2 * core
    other_y = 1 - y
    last = owners - 1

    blocks, _, feats = tok.shape
    quarter = out.shape[2]
    per_owner = blocks // owners
    owner_rows = per_owner * BLK
    half_feats = feats // 2
    width = 2 * BLK
    piece = width // PIECES

    loads = []
    for h in range(2):
        loads.append(pltpu.make_async_copy(
            up_h.at[:, h * width:(h + 1) * width], table.at[z, h, :, :width], load_sem.at[2 * h]))
        loads.append(pltpu.make_async_copy(
            down_h.at[:, h * half_feats:(h + 1) * half_feats], table.at[z, h, :, width:], load_sem.at[2 * h + 1]))
    loads.append(pltpu.make_async_copy(tok_h, tok, load_sem.at[4]))
    loads.append(pltpu.make_async_copy(base_h, base, load_sem.at[5]))
    loads.append(pltpu.make_async_copy(apb_h, apb, load_sem.at[6]))
    loads.append(pltpu.make_async_copy(apos_h, apos, load_sem.at[7]))
    for load in (*loads[:4], *loads[6:]):
        load.start()

    barrier = pltpu.get_barrier_semaphore()

    def greet(where):
        pl.semaphore_signal(barrier, inc=1, device_id=where, device_id_type=MESH)

    greet({"tensor": sibling})
    greet({"tensor": far})
    greet({"tensor": far_sibling})
    greet({"replica": other_y})

    @pl.when(z > 0)
    def _():
        greet({"adapter": z - 1})

    @pl.when(z < last)
    def _():
        greet({"adapter": z + 1})

    for load in loads[:4]:
        load.wait()
    for load in loads[4:6]:
        load.start()
    neighbours = jnp.minimum(z, 1) + jnp.minimum(last - z, 1)
    pl.semaphore_wait(barrier, 4 + neighbours)

    def part(owner, half, p):
        return table.at[owner, half, p * piece:(p + 1) * piece, :]

    def z_copy(owner, p, to, send):
        ref = part(owner, y, p) if p < PIECES else part(owner, other_y, PIECES - 1)
        return pltpu.make_async_remote_copy(
            src_ref=ref, dst_ref=ref, send_sem=send.at[owner, p], recv_sem=z_recv.at[owner, p],
            device_id={"adapter": to}, device_id_type=MESH,
        )

    def by_y(owner, p):
        outer = jnp.logical_or(owner == 0, owner == last)
        return True if p < PIECES - 1 else jnp.logical_not(outer)

    def y_copy(owner, p, half):
        ref = part(owner, half, p)
        return pltpu.make_async_remote_copy(
            src_ref=ref, dst_ref=ref, send_sem=y_send.at[owner, p], recv_sem=y_recv.at[owner, p],
            device_id={"replica": other_y}, device_id_type=MESH,
        )

    for p in range(PIECES + 1):
        @pl.when(z == 0 if p == PIECES else z < last)
        def _():
            z_copy(z, p, z + 1, right_sem).start()

        @pl.when(z == last if p == PIECES else z > 0)
        def _():
            z_copy(z, p, z - 1, left_sem).start()

    def forward(distance, p):
        @pl.when(z == distance if p == PIECES else z >= distance)
        def _():
            owner = z - distance
            z_copy(owner, p, z - 1, right_sem).wait_recv()

            @pl.when(z < last)
            def _():
                z_copy(owner, p, z + 1, right_sem).start()
            if p < PIECES:
                @pl.when(by_y(owner, p))
                def _():
                    y_copy(owner, p, y).start()

        @pl.when(z + distance == last if p == PIECES else z + distance <= last)
        def _():
            owner = z + distance
            z_copy(owner, p, z + 1, left_sem).wait_recv()

            @pl.when(z > 0)
            def _():
                z_copy(owner, p, z - 1, left_sem).start()
            if p < PIECES:
                @pl.when(by_y(owner, p))
                def _():
                    y_copy(owner, p, y).start()

    def same(a, b):
        return 1 - jnp.minimum((a - b) * (a - b), 1)

    loads[6].wait()
    loads[7].wait()
    slot = [apos[apb[b]] for b in range(blocks)]
    owner_of = [lax.div(s, 2) for s in slot]
    place = []
    for b in range(blocks):
        before = jnp.int32(0)
        for c in range(b):
            before = before + same(owner_of[c], owner_of[b])
        place.append(owner_of[b] * per_owner + before)

    row_blocks = ROWS // BLK
    row_steps = blocks // row_blocks

    def base_piece(column, r):
        at = pl.ds(r * row_blocks, row_blocks)
        columns = pl.ds(pl.multiple_of(column * quarter, quarter), quarter)
        rows = tok[at].reshape(ROWS, feats)
        value = jnp.dot(rows, base[:, columns], preferred_element_type=jnp.float32)
        return at, value.reshape(row_blocks, BLK, quarter)

    def base_copy(src, dst, sem, to):
        return pltpu.make_async_remote_copy(
            src_ref=src, dst_ref=dst, send_sem=base_sem.at[2 * sem], recv_sem=base_sem.at[2 * sem + 1],
            device_id={"tensor": to}, device_id_type=MESH,
        )

    halves = [pl.ds(i * row_blocks, row_blocks) for i in range(row_steps)]
    far_sib_copy = [
        base_copy(sib_send.at[0, half], sib_recv.at[0, half], i, sibling) for i, half in enumerate(halves)
    ]
    x_copy = [base_copy(x_send.at[half], x_recv.at[half], row_steps + i, far) for i, half in enumerate(halves)]
    sib_copy = base_copy(sib_send.at[1], sib_recv.at[1], 2 * row_steps, sibling)

    loads[4].wait()
    loads[5].wait()

    for i in range(row_steps):
        at, value = base_piece(far_sibling, i)
        sib_send[0, at] = value.astype(jnp.bfloat16)
        far_sib_copy[i].start()
    forward(1, 0)
    for i in range(row_steps):
        at, value = base_piece(far, i)
        far_sib_copy[i].wait_recv()
        x_send[at] = (value + sib_recv[0, at].astype(jnp.float32)).astype(jnp.bfloat16)
        x_copy[i].start()
        forward(1, 1 + i)

    at, value = base_piece(sibling, 0)
    sib_send[1, at] = value.astype(jnp.bfloat16)
    for p in range(1 + row_steps, PIECES + 1):
        forward(1, p)
    for i in range(1, row_steps):
        at, value = base_piece(sibling, i)
        sib_send[1, at] = value.astype(jnp.bfloat16)
    sib_copy.start()

    parity = []
    for s in range(blocks):
        index, odd = jnp.int32(0), jnp.int32(0)
        for b in range(blocks):
            here = same(place[b], s)
            index = index + here * b
            odd = odd + here * lax.rem(slot[b], 2)
        parity.append(odd)
        toks[s] = tok[index]

    lane_half = lax.div(lax.broadcasted_iota(jnp.int32, (BLK, width), 1), BLK)

    def own_lanes(owner, k):
        odd = jnp.int32(0)
        for o in range(owners):
            odd = odd + same(owner, o) * parity[o * per_owner + k]
        return same(lane_half, odd).astype(jnp.float32)

    def rank_copy(src, dst, owner, kind, to):
        return pltpu.make_async_remote_copy(
            src_ref=src.at[owner], dst_ref=dst.at[owner],
            send_sem=rank_sem.at[2 * kind, owner], recv_sem=rank_sem.at[2 * kind + 1, owner],
            device_id={"tensor": to}, device_id_type=MESH,
        )

    pairs = per_owner // 2

    def last_copies(owner):
        return [
            pltpu.make_async_remote_copy(
                src_ref=rank_send.at[owner], dst_ref=last_recv.at[i],
                send_sem=last_sem.at[2 * i], recv_sem=last_sem.at[2 * i + 1],
                device_id={"tensor": to}, device_id_type=MESH,
            )
            for i, to in enumerate((far_sibling, far, sibling))
        ]

    def shrink(owner, in_one_step=False):
        rows = toks[pl.ds(owner * per_owner, per_owner)].reshape(owner_rows, feats)
        value = jnp.zeros((owner_rows, width), jnp.float32)
        for h in range(2):
            value = value + lax.dot_general(
                rows[:, h * half_feats:(h + 1) * half_feats], table[owner, h, :, width:],
                (((1,), (1,)), ((), ())), preferred_element_type=jnp.float32,
            )
        picked = []
        for k in range(per_owner):
            rank = value[k * BLK:(k + 1) * BLK, :] * own_lanes(owner, k)
            picked.append(rank[:, :BLK] + rank[:, BLK:])
        packed = jnp.concatenate(
            [jnp.concatenate(picked[:pairs], axis=0), jnp.concatenate(picked[pairs:], axis=0)], axis=1
        )
        rank_f32[owner] = packed
        rank_send[owner] = packed.astype(jnp.bfloat16)
        if in_one_step:
            for copy in last_copies(owner):
                copy.start()
        else:
            rank_copy(rank_send, rank_sib, owner, 0, sibling).start()

    def chip_sum(owner):
        rank_copy(rank_send, rank_sib, owner, 0, sibling).wait_recv()
        value = rank_f32[owner] + rank_sib[owner].astype(jnp.float32)
        rank_f32[owner] = value
        rank_x_send[owner] = value.astype(jnp.bfloat16)
        rank_copy(rank_x_send, rank_x, owner, 1, far).start()

    def expand(owner, in_one_step=False):
        if in_one_step:
            for copy in last_copies(owner):
                copy.wait_recv()
            value = rank_f32[owner]
            for i in range(3):
                value = value + last_recv[i].astype(jnp.float32)
        else:
            rank_copy(rank_x_send, rank_x, owner, 1, far).wait_recv()
            value = rank_f32[owner] + rank_x[owner].astype(jnp.float32)
        spread = []
        for k in range(per_owner):
            column = (k // pairs) * BLK
            rank = value[(k % pairs) * BLK:(k % pairs + 1) * BLK, column:column + BLK]
            spread.append(jnp.concatenate([rank, rank], axis=1) * own_lanes(owner, k))
        shrunk = jnp.concatenate(spread, axis=0).astype(jnp.bfloat16)
        for h in range(2):
            value = jnp.dot(shrunk, table[owner, h, :, :width], preferred_element_type=jnp.float32)
            delta[pl.ds(owner * per_owner, per_owner), :, h * width:(h + 1) * width] = value.reshape(
                per_owner, BLK, width
            )

    order = [z]
    for j in range(1, owners):
        pick = jnp.int32(0)
        for me in range(owners):
            by_distance = sorted((o for o in range(owners) if o != me), key=lambda o: abs(o - me))
            pick = jnp.where(z == me, by_distance[j - 1], pick)
        order.append(pick)

    def y_wait(owner):
        for p in range(PIECES):
            @pl.when(by_y(owner, p))
            def _():
                y_copy(owner, p, other_y).wait_recv()

    forward(2, 0)
    shrink(order[0])
    forward(2, 1)
    for i in range(row_steps):
        at, value = base_piece(t, i)
        total[at] = value
        forward(2, 2 + i)
    for p in range(2 + row_steps, PIECES + 1):
        forward(2, p)
    chip_sum(order[0])
    y_wait(order[1])
    shrink(order[1])
    sib_copy.wait_recv()
    total[...] = total[...] + sib_recv[1].astype(jnp.float32)
    forward(3, 0)
    expand(order[0])
    chip_sum(order[1])
    forward(3, 1)
    y_wait(order[2])
    shrink(order[2])
    forward(3, 2)
    expand(order[1])
    for p in range(3, PIECES + 1):
        forward(3, p)
    chip_sum(order[2])
    for i, half in enumerate(halves):
        x_copy[i].wait_recv()
        total[half] = total[half] + x_recv[half].astype(jnp.float32)
    y_wait(order[3])
    shrink(order[3], in_one_step=True)
    expand(order[2])
    expand(order[3], in_one_step=True)
    for b in range(blocks):
        out[b] = (total[b] + delta[place[b]]).astype(jnp.bfloat16)

    for copy in (*far_sib_copy, *x_copy, sib_copy, *last_copies(order[3])):
        copy.wait_send()
    for owner in order[:3]:
        rank_copy(rank_send, rank_sib, owner, 0, sibling).wait_send()
        rank_copy(rank_x_send, rank_x, owner, 1, far).wait_send()
    for owner in range(owners):
        outer = owner in (0, last)
        for p in range(PIECES + 1 if outer else PIECES):
            if p < PIECES - 1 or not outer:
                @pl.when(owner != z)
                def _():
                    y_copy(owner, p, y).wait_send()

            if p < PIECES or owner == 0:
                @pl.when(jnp.logical_and(owner <= z, z < last))
                def _():
                    z_copy(owner, p, z + 1, right_sem).wait_send()

            if p < PIECES or owner == last:
                @pl.when(jnp.logical_and(owner >= z, z > 0))
                def _():
                    z_copy(owner, p, z - 1, left_sem).wait_send()


def fused(owners, tokens, value_base_matrix, down_table, up_table, adapter_per_block, adapter_position):
    rows, feats = tokens.shape
    quarter = up_table.shape[2]
    out_columns = value_base_matrix.shape[1]
    width = 2 * BLK
    blocks = rows // BLK
    owner_rows = rows // owners
    tokens = tokens.reshape(blocks, BLK, feats)
    down_rows = down_table.transpose(0, 2, 1).reshape(width, feats)
    up_rows = up_table.reshape(width, quarter)
    by_block = (blocks, BLK, quarter)
    hbm = pl.BlockSpec(memory_space=pltpu.HBM)
    rank_shape = (owners, owner_rows // 2, width)
    dma = pltpu.SemaphoreType.DMA
    out = pl.pallas_call(
        functools.partial(kernel, owners),
        out_shape=jax.ShapeDtypeStruct(by_block, jnp.bfloat16),
        in_specs=[hbm] * 6,
        out_specs=pl.BlockSpec(memory_space=pltpu.VMEM),
        scratch_shapes=[
            pltpu.VMEM((blocks, BLK, feats), jnp.bfloat16),
            pltpu.VMEM((feats, out_columns), jnp.bfloat16),
            pltpu.VMEM((owners, 2, width, width + feats // 2), jnp.bfloat16),
            pltpu.VMEM((blocks, BLK, feats), jnp.bfloat16),
            pltpu.VMEM((2, *by_block), jnp.bfloat16),
            pltpu.VMEM((2, *by_block), jnp.bfloat16),
            pltpu.VMEM(by_block, jnp.bfloat16),
            pltpu.VMEM(by_block, jnp.bfloat16),
            pltpu.VMEM(by_block, jnp.float32),
            pltpu.VMEM(rank_shape, jnp.float32),
            pltpu.VMEM(rank_shape, jnp.bfloat16),
            pltpu.VMEM(rank_shape, jnp.bfloat16),
            pltpu.VMEM(rank_shape, jnp.bfloat16),
            pltpu.VMEM(rank_shape, jnp.bfloat16),
            pltpu.VMEM((3, *rank_shape[1:]), jnp.bfloat16),
            pltpu.VMEM(by_block, jnp.float32),
            pltpu.SMEM(adapter_per_block.shape, jnp.int32),
            pltpu.SMEM(adapter_position.shape, jnp.int32),
            dma((8,)),
            dma((owners, PIECES + 1)),
            dma((owners, PIECES + 1)),
            dma((owners, PIECES + 1)),
            dma((owners, PIECES + 1)),
            dma((owners, PIECES + 1)),
            dma((2 * (2 * rows // ROWS + 1),)),
            dma((4, owners)),
            dma((6,)),
        ],
        compiler_params=pltpu.CompilerParams(
            collective_id=0, has_side_effects=True, vmem_limit_bytes=60 * 1024 * 1024
        ),
        cost_estimate=pl.CostEstimate(
            flops=2 * rows * feats * (out_columns + width),
            bytes_accessed=2 * (rows * feats + feats * out_columns + rows * quarter),
            transcendentals=0,
        ),
    )(adapter_per_block, adapter_position, tokens, value_base_matrix, down_rows, up_rows)
    return out.reshape(rows, quarter)


def solution(mesh):
    axes = mesh.shape

    def run(tokens, value_base_matrix, down_table, up_table, adapter_per_block, adapter_position):
        fits = (
            axes["tensor"] == 4
            and axes["replica"] == 2
            and axes["adapter"] == 4
            and down_table.shape[0] == 2
            and tokens.shape[0] == 16 * BLK
            and up_table.shape[1:] == (BLK, 4 * BLK)
            and tokens.shape[1] % 512 == 0
        )
        if fits:
            return fused(
                axes["adapter"], tokens, value_base_matrix, down_table, up_table, adapter_per_block, adapter_position
            )
        return shards(tokens, value_base_matrix, down_table, up_table, adapter_per_block, adapter_position)

    return jax.shard_map(
        run,
        mesh=mesh,
        in_specs=(
            P(("replica", "adapter"), "tensor"),
            P("tensor", None),
            P("adapter", "tensor", None),
            P("adapter", None, "tensor"),
            P(("replica", "adapter")),
            P("replica"),
        ),
        out_specs=P(("replica", "adapter"), "tensor"),
        check_vma=False,
    )
```

```python
import functools

import jax
import jax.numpy as jnp
from jax import lax
from jax.experimental import pallas as pl
from jax.experimental.pallas import tpu as pltpu
from jax.sharding import PartitionSpec as P

BLK = 64
PIECES = 4
ROWS = 512
MESH = pl.DeviceIdType.MESH


def shards(
    tokens,
    value_base_matrix,
    adapter_down_table,
    adapter_up_table,
    adapter_per_block,
    adapter_position,
):
    partial_value = jnp.dot(tokens, value_base_matrix, preferred_element_type=jnp.float32)
    base_projected = lax.psum_scatter(
        partial_value.astype(jnp.bfloat16), "tensor", scatter_dimension=1, tiled=True
    ).astype(jnp.float32)
    feat_width = tokens.shape[1]
    block_count = tokens.shape[0] // BLK
    all_adapters = adapter_position.shape[0]
    output_width = adapter_up_table.shape[2]
    token_groups_list = tokens.reshape(block_count, BLK, feat_width)
    matches = adapter_per_block[:, None] == jnp.arange(all_adapters, dtype=jnp.int32)[None, :]
    slot_per_block = jnp.sum(jnp.where(matches, adapter_position[None, :], 0), axis=1)
    table_down, table_up = (
        lax.all_gather(adapter_down_table, "adapter", axis=0, tiled=True),
        lax.all_gather(adapter_up_table, "adapter", axis=0, tiled=True),
    )
    down_rows = table_down[slot_per_block]
    up_rows = table_up[slot_per_block]
    shrunk_part = jnp.einsum(
        "bnd,bdr->bnr", token_groups_list, down_rows, preferred_element_type=jnp.float32
    )
    shrunk = lax.psum(shrunk_part.astype(jnp.bfloat16), "tensor")
    adapter_update = jnp.einsum(
        "bnr,bro->bno", shrunk, up_rows, preferred_element_type=jnp.float32
    ).astype(jnp.bfloat16)
    adapter_update = lax.optimization_barrier(adapter_update.reshape(tokens.shape[0], output_width))
    return (base_projected + adapter_update.astype(jnp.float32)).astype(jnp.bfloat16)


def kernel(
    owners,
    apb_h,
    apos_h,
    tok_h,
    base_h,
    down_h,
    up_h,
    out,
    tok,
    base,
    table,
    toks,
    sib_send,
    sib_recv,
    x_send,
    x_recv,
    total,
    rank_f32,
    rank_send,
    rank_sib,
    rank_x_send,
    rank_x,
    last_recv,
    delta,
    apb,
    apos,
    load_sem,
    z_recv,
    y_recv,
    right_sem,
    left_sem,
    y_send,
    base_sem,
    rank_sem,
    last_sem,
):
    y = lax.axis_index("replica")
    z = lax.axis_index("adapter")
    t = lax.axis_index("tensor")
    core = lax.rem(t, 2)
    sibling = t + 1 - 2 * core
    far = lax.rem(t + 2, 4)
    far_sibling = far + 1 - 2 * core
    other_y = 1 - y
    last = owners - 1

    blocks, _, feats = tok.shape
    quarter = out.shape[2]
    per_owner = blocks // owners
    owner_rows = per_owner * BLK
    half_feats = feats // 2
    width = 2 * BLK
    piece = width // PIECES

    loads = []
    for h in range(2):
        loads.append(pltpu.make_async_copy(
            up_h.at[:, h * width:(h + 1) * width], table.at[z, h, :, :width], load_sem.at[2 * h]))
        loads.append(pltpu.make_async_copy(
            down_h.at[:, h * half_feats:(h + 1) * half_feats], table.at[z, h, :, width:], load_sem.at[2 * h + 1]))
    loads.append(pltpu.make_async_copy(tok_h, tok, load_sem.at[4]))
    loads.append(pltpu.make_async_copy(base_h, base, load_sem.at[5]))
    loads.append(pltpu.make_async_copy(apb_h, apb, load_sem.at[6]))
    loads.append(pltpu.make_async_copy(apos_h, apos, load_sem.at[7]))
    for load in (*loads[:4], *loads[6:]):
        load.start()

    barrier = pltpu.get_barrier_semaphore()

    def greet(where):
        pl.semaphore_signal(barrier, inc=1, device_id=where, device_id_type=MESH)

    greet({"tensor": sibling})
    greet({"tensor": far})
    greet({"tensor": far_sibling})
    greet({"replica": other_y})

    @pl.when(z > 0)
    def _():
        greet({"adapter": z - 1})

    @pl.when(z < last)
    def _():
        greet({"adapter": z + 1})

    for load in loads[:4]:
        load.wait()
    for load in loads[4:6]:
        load.start()
    neighbours = jnp.minimum(z, 1) + jnp.minimum(last - z, 1)
    pl.semaphore_wait(barrier, 4 + neighbours)

    def part(owner, half, p):
        return table.at[owner, half, p * piece:(p + 1) * piece, :]

    def z_copy(owner, p, to, send):
        ref = part(owner, y, p) if p < PIECES else part(owner, other_y, PIECES - 1)
        return pltpu.make_async_remote_copy(
            src_ref=ref, dst_ref=ref, send_sem=send.at[owner, p], recv_sem=z_recv.at[owner, p],
            device_id={"adapter": to}, device_id_type=MESH,
        )

    def by_y(owner, p):
        outer = jnp.logical_or(owner == 0, owner == last)
        return True if p < PIECES - 1 else jnp.logical_not(outer)

    def y_copy(owner, p, half):
        ref = part(owner, half, p)
        return pltpu.make_async_remote_copy(
            src_ref=ref, dst_ref=ref, send_sem=y_send.at[owner, p], recv_sem=y_recv.at[owner, p],
            device_id={"replica": other_y}, device_id_type=MESH,
        )

    for p in range(PIECES + 1):
        @pl.when(z == 0 if p == PIECES else z < last)
        def _():
            z_copy(z, p, z + 1, right_sem).start()

        @pl.when(z == last if p == PIECES else z > 0)
        def _():
            z_copy(z, p, z - 1, left_sem).start()

    def forward(distance, p):
        @pl.when(z == distance if p == PIECES else z >= distance)
        def _():
            owner = z - distance
            z_copy(owner, p, z - 1, right_sem).wait_recv()

            @pl.when(z < last)
            def _():
                z_copy(owner, p, z + 1, right_sem).start()
            if p < PIECES:
                @pl.when(by_y(owner, p))
                def _():
                    y_copy(owner, p, y).start()

        @pl.when(z + distance == last if p == PIECES else z + distance <= last)
        def _():
            owner = z + distance
            z_copy(owner, p, z + 1, left_sem).wait_recv()

            @pl.when(z > 0)
            def _():
                z_copy(owner, p, z - 1, left_sem).start()
            if p < PIECES:
                @pl.when(by_y(owner, p))
                def _():
                    y_copy(owner, p, y).start()

    def same(a, b):
        return 1 - jnp.minimum((a - b) * (a - b), 1)

    loads[6].wait()
    loads[7].wait()
    slot = [apos[apb[b]] for b in range(blocks)]
    owner_of = [lax.div(s, 2) for s in slot]
    place = []
    for b in range(blocks):
        before = jnp.int32(0)
        for c in range(b):
            before = before + same(owner_of[c], owner_of[b])
        place.append(owner_of[b] * per_owner + before)

    row_blocks = ROWS // BLK
    row_steps = blocks // row_blocks

    def base_piece(column, r):
        at = pl.ds(r * row_blocks, row_blocks)
        columns = pl.ds(pl.multiple_of(column * quarter, quarter), quarter)
        rows = tok[at].reshape(ROWS, feats)
        value = jnp.dot(rows, base[:, columns], preferred_element_type=jnp.float32)
        return at, value.reshape(row_blocks, BLK, quarter)

    def base_copy(src, dst, sem, to):
        return pltpu.make_async_remote_copy(
            src_ref=src, dst_ref=dst, send_sem=base_sem.at[2 * sem], recv_sem=base_sem.at[2 * sem + 1],
            device_id={"tensor": to}, device_id_type=MESH,
        )

    halves = [pl.ds(i * row_blocks, row_blocks) for i in range(row_steps)]
    far_sib_copy = [
        base_copy(sib_send.at[0, half], sib_recv.at[0, half], i, sibling) for i, half in enumerate(halves)
    ]
    x_copy = [base_copy(x_send.at[half], x_recv.at[half], row_steps + i, far) for i, half in enumerate(halves)]
    sib_copy = base_copy(sib_send.at[1], sib_recv.at[1], 2 * row_steps, sibling)

    loads[4].wait()
    loads[5].wait()

    for i in range(row_steps):
        at, value = base_piece(far_sibling, i)
        sib_send[0, at] = value.astype(jnp.bfloat16)
        far_sib_copy[i].start()
    forward(1, 0)
    for i in range(row_steps):
        at, value = base_piece(far, i)
        far_sib_copy[i].wait_recv()
        x_send[at] = (value + sib_recv[0, at].astype(jnp.float32)).astype(jnp.bfloat16)
        x_copy[i].start()
        forward(1, 1 + i)

    at, value = base_piece(sibling, 0)
    sib_send[1, at] = value.astype(jnp.bfloat16)
    for p in range(1 + row_steps, PIECES + 1):
        forward(1, p)
    for i in range(1, row_steps):
        at, value = base_piece(sibling, i)
        sib_send[1, at] = value.astype(jnp.bfloat16)
    sib_copy.start()

    parity = []
    for s in range(blocks):
        index, odd = jnp.int32(0), jnp.int32(0)
        for b in range(blocks):
            here = same(place[b], s)
            index = index + here * b
            odd = odd + here * lax.rem(slot[b], 2)
        parity.append(odd)
        toks[s] = tok[index]

    lane_half = lax.div(lax.broadcasted_iota(jnp.int32, (BLK, width), 1), BLK)

    def own_lanes(owner, k):
        odd = jnp.int32(0)
        for o in range(owners):
            odd = odd + same(owner, o) * parity[o * per_owner + k]
        return same(lane_half, odd).astype(jnp.float32)

    def rank_copy(src, dst, owner, kind, to):
        return pltpu.make_async_remote_copy(
            src_ref=src.at[owner], dst_ref=dst.at[owner],
            send_sem=rank_sem.at[2 * kind, owner], recv_sem=rank_sem.at[2 * kind + 1, owner],
            device_id={"tensor": to}, device_id_type=MESH,
        )

    pairs = per_owner // 2

    def last_copies(owner):
        return [
            pltpu.make_async_remote_copy(
                src_ref=rank_send.at[owner], dst_ref=last_recv.at[i],
                send_sem=last_sem.at[2 * i], recv_sem=last_sem.at[2 * i + 1],
                device_id={"tensor": to}, device_id_type=MESH,
            )
            for i, to in enumerate((far_sibling, far, sibling))
        ]

    def half_dot(owner, h):
        features = pl.ds(pl.multiple_of(h * half_feats, half_feats), half_feats)
        rows = toks[pl.ds(owner * per_owner, per_owner), :, features].reshape(owner_rows, half_feats)
        return lax.dot_general(
            rows, table[owner, h, :, width:], (((1,), (1,)), ((), ())), preferred_element_type=jnp.float32
        )

    def shrink(owner, in_one_step=False):
        value = half_dot(owner, y)
        y_wait(owner)
        value = value + half_dot(owner, other_y)
        picked = []
        for k in range(per_owner):
            rank = value[k * BLK:(k + 1) * BLK, :] * own_lanes(owner, k)
            picked.append(rank[:, :BLK] + rank[:, BLK:])
        packed = jnp.concatenate(
            [jnp.concatenate(picked[:pairs], axis=0), jnp.concatenate(picked[pairs:], axis=0)], axis=1
        )
        rank_f32[owner] = packed
        rank_send[owner] = packed.astype(jnp.bfloat16)
        if in_one_step:
            for copy in last_copies(owner):
                copy.start()
        else:
            rank_copy(rank_send, rank_sib, owner, 0, sibling).start()

    def chip_sum(owner):
        rank_copy(rank_send, rank_sib, owner, 0, sibling).wait_recv()
        value = rank_f32[owner] + rank_sib[owner].astype(jnp.float32)
        rank_f32[owner] = value
        rank_x_send[owner] = value.astype(jnp.bfloat16)
        rank_copy(rank_x_send, rank_x, owner, 1, far).start()

    def expand(owner, in_one_step=False):
        if in_one_step:
            for copy in last_copies(owner):
                copy.wait_recv()
            value = rank_f32[owner]
            for i in range(3):
                value = value + last_recv[i].astype(jnp.float32)
        else:
            rank_copy(rank_x_send, rank_x, owner, 1, far).wait_recv()
            value = rank_f32[owner] + rank_x[owner].astype(jnp.float32)
        spread = []
        for k in range(per_owner):
            column = (k // pairs) * BLK
            rank = value[(k % pairs) * BLK:(k % pairs + 1) * BLK, column:column + BLK]
            spread.append(jnp.concatenate([rank, rank], axis=1) * own_lanes(owner, k))
        shrunk = jnp.concatenate(spread, axis=0).astype(jnp.bfloat16)
        for h in range(2):
            value = jnp.dot(shrunk, table[owner, h, :, :width], preferred_element_type=jnp.float32)
            delta[pl.ds(owner * per_owner, per_owner), :, h * width:(h + 1) * width] = value.reshape(
                per_owner, BLK, width
            )

    order = [z]
    for j in range(1, owners):
        pick = jnp.int32(0)
        for me in range(owners):
            by_distance = sorted((o for o in range(owners) if o != me), key=lambda o: abs(o - me))
            pick = jnp.where(z == me, by_distance[j - 1], pick)
        order.append(pick)

    def y_wait(owner):
        for p in range(PIECES):
            @pl.when(jnp.logical_and(owner != z, by_y(owner, p)))
            def _():
                y_copy(owner, p, other_y).wait_recv()

    forward(2, 0)
    shrink(order[0])
    forward(2, 1)
    for i in range(row_steps):
        at, value = base_piece(t, i)
        total[at] = value
        forward(2, 2 + i)
    for p in range(2 + row_steps, PIECES + 1):
        forward(2, p)
    chip_sum(order[0])
    shrink(order[1])
    sib_copy.wait_recv()
    total[...] = total[...] + sib_recv[1].astype(jnp.float32)
    forward(3, 0)
    expand(order[0])
    chip_sum(order[1])
    forward(3, 1)
    shrink(order[2])
    forward(3, 2)
    expand(order[1])
    for p in range(3, PIECES + 1):
        forward(3, p)
    chip_sum(order[2])
    for i, half in enumerate(halves):
        x_copy[i].wait_recv()
        total[half] = total[half] + x_recv[half].astype(jnp.float32)
    shrink(order[3], in_one_step=True)
    expand(order[2])
    expand(order[3], in_one_step=True)
    for b in range(blocks):
        out[b] = (total[b] + delta[place[b]]).astype(jnp.bfloat16)

    for copy in (*far_sib_copy, *x_copy, sib_copy, *last_copies(order[3])):
        copy.wait_send()
    for owner in order[:3]:
        rank_copy(rank_send, rank_sib, owner, 0, sibling).wait_send()
        rank_copy(rank_x_send, rank_x, owner, 1, far).wait_send()
    for owner in range(owners):
        outer = owner in (0, last)
        for p in range(PIECES + 1 if outer else PIECES):
            if p < PIECES - 1 or not outer:
                @pl.when(owner != z)
                def _():
                    y_copy(owner, p, y).wait_send()

            if p < PIECES or owner == 0:
                @pl.when(jnp.logical_and(owner <= z, z < last))
                def _():
                    z_copy(owner, p, z + 1, right_sem).wait_send()

            if p < PIECES or owner == last:
                @pl.when(jnp.logical_and(owner >= z, z > 0))
                def _():
                    z_copy(owner, p, z - 1, left_sem).wait_send()


def fused(owners, tokens, value_base_matrix, down_table, up_table, adapter_per_block, adapter_position):
    rows, feats = tokens.shape
    quarter = up_table.shape[2]
    out_columns = value_base_matrix.shape[1]
    width = 2 * BLK
    blocks = rows // BLK
    owner_rows = rows // owners
    tokens = tokens.reshape(blocks, BLK, feats)
    down_rows = down_table.transpose(0, 2, 1).reshape(width, feats)
    up_rows = up_table.reshape(width, quarter)
    by_block = (blocks, BLK, quarter)
    hbm = pl.BlockSpec(memory_space=pltpu.HBM)
    rank_shape = (owners, owner_rows // 2, width)
    dma = pltpu.SemaphoreType.DMA
    out = pl.pallas_call(
        functools.partial(kernel, owners),
        out_shape=jax.ShapeDtypeStruct(by_block, jnp.bfloat16),
        in_specs=[hbm] * 6,
        out_specs=pl.BlockSpec(memory_space=pltpu.VMEM),
        scratch_shapes=[
            pltpu.VMEM((blocks, BLK, feats), jnp.bfloat16),
            pltpu.VMEM((feats, out_columns), jnp.bfloat16),
            pltpu.VMEM((owners, 2, width, width + feats // 2), jnp.bfloat16),
            pltpu.VMEM((blocks, BLK, feats), jnp.bfloat16),
            pltpu.VMEM((2, *by_block), jnp.bfloat16),
            pltpu.VMEM((2, *by_block), jnp.bfloat16),
            pltpu.VMEM(by_block, jnp.bfloat16),
            pltpu.VMEM(by_block, jnp.bfloat16),
            pltpu.VMEM(by_block, jnp.float32),
            pltpu.VMEM(rank_shape, jnp.float32),
            pltpu.VMEM(rank_shape, jnp.bfloat16),
            pltpu.VMEM(rank_shape, jnp.bfloat16),
            pltpu.VMEM(rank_shape, jnp.bfloat16),
            pltpu.VMEM(rank_shape, jnp.bfloat16),
            pltpu.VMEM((3, *rank_shape[1:]), jnp.bfloat16),
            pltpu.VMEM(by_block, jnp.float32),
            pltpu.SMEM(adapter_per_block.shape, jnp.int32),
            pltpu.SMEM(adapter_position.shape, jnp.int32),
            dma((8,)),
            dma((owners, PIECES + 1)),
            dma((owners, PIECES + 1)),
            dma((owners, PIECES + 1)),
            dma((owners, PIECES + 1)),
            dma((owners, PIECES + 1)),
            dma((2 * (2 * rows // ROWS + 1),)),
            dma((4, owners)),
            dma((6,)),
        ],
        compiler_params=pltpu.CompilerParams(
            collective_id=0, has_side_effects=True, vmem_limit_bytes=60 * 1024 * 1024
        ),
        cost_estimate=pl.CostEstimate(
            flops=2 * rows * feats * (out_columns + width),
            bytes_accessed=2 * (rows * feats + feats * out_columns + rows * quarter),
            transcendentals=0,
        ),
    )(adapter_per_block, adapter_position, tokens, value_base_matrix, down_rows, up_rows)
    return out.reshape(rows, quarter)


def solution(mesh):
    axes = mesh.shape

    def run(tokens, value_base_matrix, down_table, up_table, adapter_per_block, adapter_position):
        fits = (
            axes["tensor"] == 4
            and axes["replica"] == 2
            and axes["adapter"] == 4
            and down_table.shape[0] == 2
            and tokens.shape[0] == 16 * BLK
            and up_table.shape[1:] == (BLK, 4 * BLK)
            and tokens.shape[1] % 512 == 0
        )
        if fits:
            return fused(
                axes["adapter"], tokens, value_base_matrix, down_table, up_table, adapter_per_block, adapter_position
            )
        return shards(tokens, value_base_matrix, down_table, up_table, adapter_per_block, adapter_position)

    return jax.shard_map(
        run,
        mesh=mesh,
        in_specs=(
            P(("replica", "adapter"), "tensor"),
            P("tensor", None),
            P("adapter", "tensor", None),
            P("adapter", None, "tensor"),
            P(("replica", "adapter")),
            P("replica"),
        ),
        out_specs=P(("replica", "adapter"), "tensor"),
        check_vma=False,
    )
```
